32 devices in a mesh: groups: 2 (over x), seq: 16 (over z, y, core).
Axes of the slice: x: 2, y: 2, z: 4, core: 2. Of those that a mesh axis runs over, the one named last changes fastest.
Arguments:
- q_latent: bfloat16 [2, 32, 1536], P(None, ('groups', 'seq')), parts along dimension 1, may hold values from -17.5 to 17.5
- latent_cache: bfloat16 [1536, 16, 576], P(('groups', 'seq')), parts along dimension 0, may hold values from -14 to 14
- block_table: int32 [32, 48], P(('groups', 'seq')), parts along dimension 0, may hold values from 0 to 767, as said below
- lengths: int32 [32], P(('groups', 'seq')), parts along dimension 0, may hold values from 48 to 766, as said below
- query_up: bfloat16 [1536, 24576], P(None, 'seq'), may hold values from -0.15625 to 0.15625
- key_up: bfloat16 [128, 128, 512], P('seq'), may hold values from -0.25 to 0.25
- value_up: bfloat16 [128, 512, 128], P('seq'), may hold values from -2 to 2
- output_weight: bfloat16 [16384, 7168], P('seq'), may hold values from -0.046875 to 0.046875
Outputs:
- attn_out: bfloat16 [2, 32, 7168], P(None, ('groups', 'seq')), parts along dimension 1
The draws below stay inside these ranges and needn't reach their ends.
There are 2 independent parts, one for each index of `groups`. The reference program is written for one: setup_inputs(seed, part) draws one part's arguments, and reference() takes and returns one part's arrays. A program takes and returns all parts, laid end to end along the dimension named above; an argument that names none is the same for every part. Nothing has to cross between parts.
Inputs may be any that keep to these rules, and one draw needn't show every extreme that they name: `block_table`: every entry names one parked block (it is parked on seq device id // 48, at row id % 48 there), and every parked block is named exactly once. Along the rows of one resuming device (its trajectories one after another, slots in order) the slots fall in runs of 3 consecutive slots naming blocks of one parking device, and every parking device gives exactly one such run to every resuming device. `lengths`: some trajectory reaches the largest value in every draw.
All inputs are finite; a program needn't handle non-finite values.
Results may differ from the reference program's by a relative error of at most 0.009.
The reference program's roundings to bfloat16 on the way (of `query`, `absorbed`, `rotated`, `key`, `weights`, `latent_out` and `values`) count: a program that leaves them out, or rounds other values in their place, can miss the bound.
Values may be sent and summed in bfloat16 or wider, within the bound.
A program may use at most 128 MiB of HBM per device.

```python
import math
import jax
import jax.numpy as jnp
from jax import lax

D = 7168
HEADS = 128
QL = 1536
LAT = 512
ROPE = 64
NOPE = 128
VDIM = 128
BLOCK = 16
CAP = 3
STEPS = 2
TRAJS = 16
PARKED_DEV = 48
PARKED = 768
SLOTS = 48
MAX_LEN = 768
N_SEQ = 16


def local_permutation(subkey):
    return jax.random.permutation(subkey, PARKED_DEV)


def draw_block_table(key, part):
    key_parkers, key_offsets, key_local = jax.random.split(key, 3)
    parker_order = jax.random.permutation(key_parkers, N_SEQ).astype(jnp.int32)
    offset_order = jax.random.permutation(key_offsets, N_SEQ).astype(jnp.int32)
    local_order = jax.vmap(local_permutation)(jax.random.split(key_local, N_SEQ)).astype(jnp.int32)
    resumer = jnp.arange(N_SEQ, dtype=jnp.int32)[:, None]
    slot_index = jnp.arange(CAP * N_SEQ, dtype=jnp.int32)[None, :]
    run_index = slot_index // CAP
    within_run = slot_index % CAP
    parker = parker_order[(offset_order[resumer] + run_index) % N_SEQ]
    local_row = local_order[parker, resumer * CAP + within_run]
    table = parker * PARKED_DEV + local_row
    return table.reshape(TRAJS, SLOTS).astype(jnp.int32)


def draw_lengths(key, part):
    key_values, key_pick = jax.random.split(key)
    drawn = jax.random.randint(key_values, (TRAJS,), CAP * BLOCK, MAX_LEN - 1, dtype=jnp.int32)
    chosen = jax.random.randint(key_pick, (), 0, TRAJS, dtype=jnp.int32)
    return jnp.where(jnp.arange(TRAJS, dtype=jnp.int32) == chosen, MAX_LEN - 2, drawn).astype(jnp.int32)


def draw_q_latent(key, part):
    return jnp.clip(jax.random.normal(key, (STEPS, TRAJS, QL), jnp.float32), -6.0, 6.0).astype(jnp.bfloat16)


def draw_latent_cache(key, part):
    return jnp.clip(jax.random.normal(key, (PARKED, BLOCK, LAT + ROPE), jnp.float32), -6.0, 6.0).astype(jnp.bfloat16)


def block_levels(key, shape, pieces, low, top_value):
    def one(dim, blocks):
        heights = jax.random.uniform(jax.random.fold_in(jax.random.fold_in(key, 6), dim), (blocks,), jnp.float32, low / len(pieces), top_value / len(pieces))
        return jnp.repeat(jnp.exp(heights), shape[dim] // blocks).reshape((-1,) + (1,) * (len(shape) - dim - 1))

    loudness = one(*pieces[0])
    for cut in pieces[1:]:
        loudness = loudness * one(*cut)
    return loudness


def scatter_about(stream_key, extent, scale, bound, cuts=(), kind=jnp.bfloat16):
    entries = scale * jax.random.normal(stream_key, extent, jnp.float32)
    if cuts:
        entries = entries * block_levels(stream_key, extent, cuts, -0.22, 0.18)
    return jnp.clip(entries, -bound, bound).astype(kind)


def setup_inputs(seed: int = 0, part: int = 0) -> dict:
    seeds = jax.random.split(jax.random.key(seed), 9)
    part_keys = jax.random.split(jax.random.fold_in(seeds[8], part), 9)
    q_latent = draw_q_latent(jax.random.fold_in(jax.random.fold_in(seeds[8], part), 71), part)
    latent_cache = draw_latent_cache(jax.random.fold_in(jax.random.fold_in(seeds[8], part), 71), part)
    block_table = draw_block_table(jax.random.fold_in(jax.random.fold_in(seeds[8], part), 71), part)
    lengths = draw_lengths(jax.random.fold_in(jax.random.fold_in(seeds[8], part), 71), part)
    query_up = scatter_about(seeds[4], (QL, HEADS * (NOPE + ROPE)), QL ** -0.5, 0.15625, ((1, 16),))
    key_up = scatter_about(seeds[5], (HEADS, NOPE, LAT), LAT ** -0.5, 0.25, ((0, 16),))
    value_up = scatter_about(seeds[6], (HEADS, LAT, VDIM), (max(LAT // 64, 1)) ** -0.5, 2.0, ((0, 16),))
    output_weight = scatter_about(seeds[7], (HEADS * VDIM, D), (HEADS * VDIM) ** -0.5, 0.046875, ((0, 16),))
    return dict(q_latent=q_latent, latent_cache=latent_cache, block_table=block_table, lengths=lengths, query_up=query_up, key_up=key_up, value_up=value_up, output_weight=output_weight)


softmax_scale = 0.13524
big_negative = -1e30


def frequencies(half_width):
    return jnp.exp(-math.log(10000.0) * jnp.arange(half_width, dtype=jnp.float32) / half_width)


def rotate(q_rope, angle):
    half_width = q_rope.shape[-1] // 2
    upper = q_rope[..., :half_width]
    lower = q_rope[..., half_width:]
    cosine = jnp.cos(angle)
    sine_part = jnp.sin(angle)
    return jnp.concatenate([upper * cosine - lower * sine_part, upper * sine_part + lower * cosine], axis=-1)


def reference(q_latent, latent_cache, block_table, lengths, query_up, key_up, value_up, output_weight):
    query = jnp.dot(q_latent.reshape(STEPS * TRAJS, QL), query_up, preferred_element_type=jnp.float32)
    query = query.astype(jnp.bfloat16).reshape(STEPS, TRAJS, HEADS, NOPE + ROPE)
    absorbed = jnp.einsum("sbhn,hnl->sbhl", query[..., :NOPE].astype(jnp.float32), key_up.astype(jnp.float32)).astype(jnp.bfloat16)
    q_rope = query[..., NOPE:]
    inverse = frequencies(ROPE // 2)
    step_offsets = jnp.arange(STEPS, dtype=jnp.int32)
    key_positions = jnp.arange(SLOTS * BLOCK, dtype=jnp.int32)

    def attend_one(packed):
        block_ids, length_one, absorbed_one, rope_one = packed
        keys = jnp.take(latent_cache, block_ids, axis=0).reshape(SLOTS * BLOCK, LAT + ROPE)
        position = length_one + step_offsets
        angle = position.astype(jnp.float32)[:, None, None] * inverse
        rotated = rotate(rope_one.astype(jnp.float32), angle).astype(jnp.bfloat16)
        q_full = jnp.concatenate([absorbed_one, rotated], axis=-1)
        scores = jnp.einsum("shw,kw->shk", q_full.astype(jnp.float32), keys.astype(jnp.float32)) * softmax_scale
        keep = key_positions[None, None, :] <= position[:, None, None]
        scores = jnp.where(keep, scores, big_negative)
        highest = jnp.max(scores, axis=-1, keepdims=True)
        expo_terms = jnp.exp(scores - highest)
        weights = (expo_terms / jnp.sum(expo_terms, axis=-1, keepdims=True)).astype(jnp.bfloat16)
        latent_out = jnp.einsum("shk,kl->shl", weights.astype(jnp.float32), keys[:, :LAT].astype(jnp.float32))
        return latent_out.astype(jnp.bfloat16)

    latent_out = lax.map(attend_one, (block_table, lengths, absorbed.transpose(1, 0, 2, 3), q_rope.transpose(1, 0, 2, 3)))
    values = jnp.einsum("bshl,hlv->bshv", latent_out.astype(jnp.float32), value_up.astype(jnp.float32)).astype(jnp.bfloat16)
    result = jnp.dot(values.reshape(TRAJS * STEPS, HEADS * VDIM), output_weight, preferred_element_type=jnp.float32)
    return result.reshape(TRAJS, STEPS, D).transpose(1, 0, 2).astype(jnp.bfloat16)
```

```python
import functools
import math

import jax
import jax.numpy as jnp
from jax import lax
from jax.experimental import pallas as pl
from jax.experimental.pallas import tpu as pltpu
from jax.sharding import PartitionSpec as P

softmax_scale = 0.13524
big_negative = -1e30
F32 = jnp.float32
BF16 = jnp.bfloat16
MESH = pl.DeviceIdType.MESH


def kernel(
    n, hl, cap, chunks,
    q_ref, cache_hbm, tab_ref, tab_smem, len_smem, rot_ref, qup_hbm, kup_hbm, vup_hbm, ow_hbm,
    out_ref,
    qup, kup, vup, ow, tabs, idx_v, idx_s, q_own, q_all, q_tmp, stage, keys,
    pack, q_send, q_recv, l_send, l_recv, part_in, rs_send, rs_recv,
    w_sem, idx_sem, s_sem, r_sem, pair_s, pair_r,
):
    me = lax.axis_index("seq")
    group = lax.axis_index("groups")
    steps = 2
    width = cache_hbm.shape[2]
    latent = kup.shape[2]
    nope = kup.shape[1]
    head_w = nope + width - latent
    block = cache_hbm.shape[1]
    parked = cache_hbm.shape[0]
    slots = tab_ref.shape[1]
    rows = q_send.shape[1]
    half = n // 2
    cols = part_in.shape[2]
    run = cap * block
    toks = n * run
    qcols = q_ref.shape[2] // 128
    core = lax.rem(me, 2)
    pair = me + 1 - 2 * core

    loads = [
        pltpu.make_async_copy(qup_hbm, qup, w_sem.at[1]),
        pltpu.make_async_copy(kup_hbm, kup, w_sem.at[2]),
        pltpu.make_async_copy(vup_hbm, vup, w_sem.at[3]),
        pltpu.make_async_copy(ow_hbm, ow, w_sem.at[4]),
    ]

    def send(src, dst, phase, to):
        pltpu.make_async_remote_copy(
            src_ref=src, dst_ref=dst, send_sem=s_sem.at[phase], recv_sem=r_sem.at[phase],
            device_id=(group, to), device_id_type=MESH,
        ).start()

    def bulk(buf, count, sem):
        piece = buf.at[pl.ds(0, count)]
        pltpu.make_async_copy(piece, piece, sem).wait()

    def first_part(cache):
        cache_load = pltpu.make_async_copy(cache_hbm, cache, w_sem.at[0])
        cache_load.start()
        for load in loads:
            load.start()

        barrier = pltpu.get_barrier_semaphore()

        def greet(k, carry):
            pl.semaphore_signal(
                barrier, inc=1, device_id=(group, lax.rem(me + k, n)), device_id_type=MESH
            )
            return carry

        lax.fori_loop(1, n, greet, 0)

        tabs[me] = jnp.full((1, tabs.shape[2]), -1, jnp.int32)
        tabs[me, :, 0:slots] = tab_ref[...]
        q_tmp[0] = jnp.zeros_like(q_tmp[0])
        for s in range(steps):
            row = q_ref[s].astype(F32)
            for c in range(qcols):
                r = s * qcols + c
                q_tmp[0, r : r + 1, :] = row[:, c * 128 : (c + 1) * 128]
        q_own[...] = q_tmp[0].astype(BF16)
        q_all[me] = q_own[...]

        pl.semaphore_wait(barrier, n - 1)

        def send_small(k, carry):
            to = lax.rem(me + k, n)
            send(tabs.at[me], tabs.at[me], 0, to)
            return carry

        lax.fori_loop(1, n, send_small, 0)

        def send_query(k, carry):
            to = lax.rem(me + k, n)
            send(q_own, q_all.at[me], 1, to)
            return carry

        lax.fori_loop(1, n, send_query, 0)

        bulk(tabs, n - 1, r_sem.at[0])
        table = tabs[...].reshape(n, tabs.shape[2])
        lane = lax.broadcasted_iota(jnp.int32, table.shape, 1)
        within = lane - cap * ((lane * 21846) >> 16)
        local = table - me * parked
        mine = (local >= 0) & (local < parked)
        out_lane = lax.broadcasted_iota(jnp.int32, (n, 128), 1)
        wanted = jnp.zeros((n, 128), jnp.int32)
        for c in range(cap):
            picked = jnp.sum(jnp.where(mine & (within == c), local, 0), axis=1, keepdims=True)
            wanted = jnp.where(out_lane == c, picked, wanted)
        idx_v[...] = wanted
        fetch = pltpu.make_async_copy(idx_v, idx_s, idx_sem)
        fetch.start()
        fetch.wait()
        cache_load.wait()

        for c in range(cap):
            keys[me, c * block : (c + 1) * block, :] = cache[idx_s[me, c]]

        def send_blocks(k, carry):
            to = lax.rem(me + k, n)
            for c in range(cap):
                stage[to, c * block : (c + 1) * block, :] = cache[idx_s[to, c]]
            send(stage.at[to], keys.at[me], 2, to)
            return carry

        lax.fori_loop(1, n, send_blocks, 0)

    pl.run_scoped(first_part, pltpu.VMEM(cache_hbm.shape, BF16))

    bulk(q_all, n - 1, r_sem.at[1])
    q_tmp[...] = q_all[...].astype(F32)
    latents = jnp.concatenate(
        [
            jnp.concatenate([q_tmp[:, s * qcols + c, :] for c in range(qcols)], axis=1)
            for s in range(steps)
        ],
        axis=0,
    ).astype(BF16)
    loads[0].wait()
    query = jnp.dot(latents, qup[...], preferred_element_type=F32).astype(BF16).astype(F32)
    loads[1].wait()
    if rows != steps * hl:
        pack[...] = jnp.zeros_like(pack)
    for h in range(hl):
        at = h * head_w
        absorbed = jnp.dot(
            query[:, at : at + nope].astype(BF16), kup[h], preferred_element_type=F32
        )
        for s in range(steps):
            pack[:, s * hl + h, 0:latent] = absorbed[s * n : (s + 1) * n]
            pack[:, s * hl + h, latent:width] = query[s * n : (s + 1) * n, at + nope : at + head_w]
    q_recv[me] = pack[me].astype(BF16)

    def send_absorbed(k, carry):
        to = lax.rem(me + k, n)
        q_send[to] = pack[to].astype(BF16)
        send(q_send.at[to], q_recv.at[me], 3, to)
        return carry

    lax.fori_loop(1, n, send_absorbed, 0)

    token = lax.broadcasted_iota(jnp.int32, (1, toks), 1)

    def place(k, position):
        first = tab_smem[0, cap * k] // parked * run
        inside = (token >= first) & (token < first + run)
        return jnp.where(inside, token - first + k * run, position)

    position = lax.fori_loop(0, n, place, token)

    bulk(q_recv, n - 1, r_sem.at[3])
    bulk(keys, n - 1, r_sem.at[2])

    owners = max(256 // n, 1)
    group_rows = owners * rows
    row_in = lax.broadcasted_iota(jnp.int32, (group_rows, 1), 0) & (rows - 1)
    second = row_in >= hl
    last = len_smem[0] + second.astype(jnp.int32)
    cosine = jnp.where(second, rot_ref[1:2, :], rot_ref[0:1, :])
    sine = jnp.where(second, rot_ref[3:4, :], rot_ref[2:3, :])
    quarter = (width - latent) // 2

    def attend(i, carry):
        q = q_recv[pl.ds(i * owners, owners)].reshape(group_rows, width)
        kv = keys[...].reshape(toks, width)
        x = q[:, latent:].astype(F32)
        swapped = jnp.concatenate([x[:, quarter:], x[:, :quarter]], axis=1)
        rotated = (x * cosine + swapped * sine).astype(BF16)
        full = jnp.concatenate([q[:, :latent], rotated], axis=1)
        scores = lax.dot_general(
            full, kv, (((1,), (1,)), ((), ())), preferred_element_type=F32
        ) * softmax_scale
        scores = jnp.where(position <= last, scores, big_negative)
        terms = jnp.exp(scores - jnp.max(scores, axis=1, keepdims=True))
        weights = (terms / jnp.sum(terms, axis=1, keepdims=True)).astype(BF16)
        result = jnp.dot(weights, kv[:, :latent], preferred_element_type=F32).astype(BF16)
        l_send[pl.ds(i * owners, owners)] = result.reshape(owners, rows, latent)
        return carry

    lax.fori_loop(0, n // owners, attend, 0)

    l_recv[me] = l_send[me]

    def send_latent(k, carry):
        to = lax.rem(me + k, n)
        send(l_send.at[to], l_recv.at[me], 4, to)
        return carry

    lax.fori_loop(1, n, send_latent, 0)
    bulk(l_recv, n - 1, r_sem.at[4])
    pack[:, :, 0:latent] = l_recv[...].astype(F32)
    loads[2].wait()

    def per_head(h):
        taken = jnp.concatenate(
            [pack[:, s * hl + h, 0:latent] for s in range(steps)], axis=0
        ).astype(BF16)
        return jnp.dot(taken, vup[h], preferred_element_type=F32)

    values = jnp.concatenate([per_head(h) for h in range(hl)], axis=1)
    wide = values.shape[1]
    both = jnp.stack([values[:n], values[n:]], axis=1)
    both = both.reshape(half, 2, 2, wide)
    both = jnp.concatenate([both[:, 0], both[:, 1]], axis=0).reshape(2 * n, wide)
    values = both.astype(BF16)
    loads[3].wait()

    chip = me // 2

    def last_part(part):
        def pair_copy(j):
            return pltpu.make_async_remote_copy(
                src_ref=part.at[j, pl.ds(pl.multiple_of((1 - core) * n, 8), n)],
                dst_ref=part_in.at[j],
                send_sem=pair_s.at[j], recv_sem=pair_r.at[j],
                device_id=(group, pair), device_id_type=MESH,
            )

        def project(j, carry):
            @pl.when(j < chunks)
            def _():
                at = pl.multiple_of(j * cols, 128)
                part[j] = jnp.dot(values, ow[:, pl.ds(at, cols)], preferred_element_type=F32)
                pair_copy(j).start()

            @pl.when(j > 0)
            def _():
                i = j - 1
                pair_copy(i).wait_recv()
                own = part[i, pl.ds(pl.multiple_of(core * n, 8), n)] + part_in[i]
                rs_send[i] = own.reshape(half, 2, cols)
                rs_recv[chip, i] = rs_send[i, chip]

                def scatter(k, c2):
                    to = lax.rem(chip + k, half)
                    send(rs_send.at[i, to], rs_recv.at[chip, i], 5, 2 * to + core)
                    return c2

                lax.fori_loop(1, half, scatter, 0)

            return carry

        lax.fori_loop(0, chunks + 1, project, 0)
        for j in range(chunks):
            pair_copy(j).wait_send()

    pl.run_scoped(last_part, pltpu.VMEM((chunks, 2 * n, cols), F32))

    bulk(rs_recv, half - 1, r_sem.at[5])
    for j in range(chunks):
        total = rs_recv[0, j]
        for k in range(1, half):
            total = total + rs_recv[k, j]
        out_ref[:, j * cols : (j + 1) * cols] = total.astype(BF16)

    bulk(tabs, n - 1, s_sem.at[0])
    bulk(q_all, n - 1, s_sem.at[1])
    bulk(stage, n - 1, s_sem.at[2])
    bulk(q_send, n - 1, s_sem.at[3])
    bulk(l_send, n - 1, s_sem.at[4])
    bulk(rs_recv, half - 1, s_sem.at[5])


def frequencies(half_width):
    return jnp.exp(-math.log(10000.0) * jnp.arange(half_width, dtype=F32) / half_width)


def on_device(
    q_latent, latent_cache, block_table, lengths, query_up, key_up, value_up, output_weight
):
    n = lax.axis_size("seq")
    steps, _, ql = q_latent.shape
    parked, block, width = latent_cache.shape
    slots = block_table.shape[1]
    hl, nope, latent = key_up.shape
    vdim = value_up.shape[2]
    d = output_weight.shape[1]
    cap = parked // n
    rows = -(-steps * hl // 16) * 16
    tab_w = -(-slots // 128) * 128
    q_rows = -(-steps * ql // 128 // 16) * 16
    chunks = 7
    cols = d // chunks
    half = n // 2
    run = cap * block

    position = lengths[0] + jnp.arange(steps, dtype=jnp.int32)
    angle = position.astype(F32)[:, None] * frequencies((width - latent) // 2)
    cosine, sine = jnp.cos(angle), jnp.sin(angle)
    rot = jnp.concatenate(
        [
            jnp.concatenate([cosine, cosine], axis=1),
            jnp.concatenate([-sine, sine], axis=1),
        ],
        axis=0,
    )
    vmem = pl.BlockSpec(memory_space=pltpu.VMEM)
    smem = pl.BlockSpec(memory_space=pltpu.SMEM)
    hbm = pl.BlockSpec(memory_space=pl.ANY)
    out = pl.pallas_call(
        functools.partial(kernel, n, hl, cap, chunks),
        out_shape=jax.ShapeDtypeStruct((steps, d), BF16),
        in_specs=[vmem, hbm, vmem, smem, smem, vmem, hbm, hbm, hbm, hbm],
        out_specs=vmem,
        scratch_shapes=[
            pltpu.VMEM(query_up.shape, BF16),
            pltpu.VMEM(key_up.shape, BF16),
            pltpu.VMEM(value_up.shape, BF16),
            pltpu.VMEM(output_weight.shape, BF16),
            pltpu.VMEM((n, 1, tab_w), jnp.int32),
            pltpu.VMEM((n, 128), jnp.int32),
            pltpu.SMEM((n, 128), jnp.int32),
            pltpu.VMEM((q_rows, 128), BF16),
            pltpu.VMEM((n, q_rows, 128), BF16),
            pltpu.VMEM((n, q_rows, 128), F32),
            pltpu.VMEM((n, run, width), BF16),
            pltpu.VMEM((n, run, width), BF16),
            pltpu.VMEM((n, rows, width), F32),
            pltpu.VMEM((n, rows, width), BF16),
            pltpu.VMEM((n, rows, width), BF16),
            pltpu.VMEM((n, rows, latent), BF16),
            pltpu.VMEM((n, rows, latent), BF16),
            pltpu.VMEM((chunks, n, cols), F32),
            pltpu.VMEM((chunks, half, steps, cols), F32),
            pltpu.VMEM((half, chunks, steps, cols), F32),
            pltpu.SemaphoreType.DMA((5,)),
            pltpu.SemaphoreType.DMA,
            pltpu.SemaphoreType.DMA((6,)),
            pltpu.SemaphoreType.DMA((6,)),
            pltpu.SemaphoreType.DMA((chunks,)),
            pltpu.SemaphoreType.DMA((chunks,)),
        ],
        compiler_params=pltpu.CompilerParams(
            collective_id=0, has_side_effects=True, vmem_limit_bytes=61 * 1024 * 1024
        ),
    )(
        q_latent, latent_cache, block_table, block_table, lengths, rot,
        query_up, key_up, value_up, output_weight,
    )
    return out[:, None, :]


def solution(mesh):
    in_specs = (
        P(None, ("groups", "seq"), None),
        P(("groups", "seq"), None, None),
        P(("groups", "seq"), None),
        P(("groups", "seq")),
        P(None, "seq"),
        P("seq", None, None),
        P("seq", None, None),
        P("seq", None),
    )
    out_specs = P(None, ("groups", "seq"), None)
    return jax.shard_map(
        on_device, mesh=mesh, in_specs=in_specs, out_specs=out_specs, check_vma=False
    )
```

```python
import functools
import math

import jax
import jax.numpy as jnp
from jax import lax
from jax.experimental import pallas as pl
from jax.experimental.pallas import tpu as pltpu
from jax.sharding import PartitionSpec as P

softmax_scale = 0.13524
big_negative = -1e30
F32 = jnp.float32
BF16 = jnp.bfloat16
MESH = pl.DeviceIdType.MESH


def kernel(
    n, hl, cap, chunks,
    q_ref, cache_hbm, tab_ref, tab_smem, len_smem, qup_hbm, kup_hbm, vup_hbm, ow_hbm,
    out_ref,
    qup, kup, vup, ow, tabs, idx_v, idx_s, q_own, q_all, q_tmp, stage, keys,
    pack, q_send, q_recv, l_send, l_recv, part_in, mid_in, rs_send, rs_recv,
    w_sem, idx_sem, s_sem, r_sem, pair_s, pair_r, mid_s, mid_r,
):
    me = lax.axis_index("seq")
    group = lax.axis_index("groups")
    steps = 2
    width = cache_hbm.shape[2]
    latent = kup.shape[2]
    nope = kup.shape[1]
    head_w = nope + width - latent
    block = cache_hbm.shape[1]
    parked = cache_hbm.shape[0]
    slots = tab_ref.shape[1]
    rows = q_send.shape[1]
    half = n // 2
    cols = part_in.shape[2]
    run = cap * block
    toks = n * run
    qcols = q_ref.shape[1] // 128
    core = lax.rem(me, 2)
    pair = me + 1 - 2 * core
    planes = n // 4
    low, hi = lax.rem(me, 4), me // 4
    side, inside_side = me // half, lax.rem(me, half)

    def place_of(device):
        return lax.rem(device, 4) * planes + device // 4


    loads = [
        pltpu.make_async_copy(qup_hbm, qup, w_sem.at[1]),
        pltpu.make_async_copy(kup_hbm, kup, w_sem.at[2]),
        pltpu.make_async_copy(vup_hbm, vup, w_sem.at[3]),
        pltpu.make_async_copy(ow_hbm, ow, w_sem.at[4]),
    ]

    def send(src, dst, phase, to):
        pltpu.make_async_remote_copy(
            src_ref=src, dst_ref=dst, send_sem=s_sem.at[phase], recv_sem=r_sem.at[phase],
            device_id=(group, to), device_id_type=MESH,
        ).start()

    def bulk(buf, count, sem):
        piece = buf.at[pl.ds(0, count)]
        pltpu.make_async_copy(piece, piece, sem).wait()

    def first_part(cache):
        cache_load = pltpu.make_async_copy(cache_hbm, cache, w_sem.at[0])
        cache_load.start()
        for load in loads:
            load.start()

        barrier = pltpu.get_barrier_semaphore()

        def greet(k, carry):
            pl.semaphore_signal(
                barrier, inc=1, device_id=(group, lax.rem(me + k, n)), device_id_type=MESH
            )
            return carry

        lax.fori_loop(1, n, greet, 0)

        tabs[me] = jnp.full((1, tabs.shape[2]), -1, jnp.int32)
        tabs[me, :, 0:slots] = tab_ref[...]
        q_tmp[0] = jnp.zeros_like(q_tmp[0])
        for s in range(steps):
            row = q_ref[s : s + 1, :].astype(F32)
            for c in range(qcols):
                r = s * qcols + c
                q_tmp[0, r : r + 1, :] = row[:, c * 128 : (c + 1) * 128]
        q_own[...] = q_tmp[0].astype(BF16)
        q_all[place_of(me)] = q_own[...]

        pl.semaphore_wait(barrier, n - 1)

        def send_small(k, carry):
            to = lax.rem(me + k, n)
            send(tabs.at[me], tabs.at[me], 0, to)
            return carry

        lax.fori_loop(1, n, send_small, 0)

        def send_query(k, carry):
            to = 4 * lax.rem(hi + k, planes) + low
            send(q_own, q_all.at[place_of(me)], 1, to)
            return carry

        lax.fori_loop(1, planes, send_query, 0)

        bulk(tabs, n - 1, r_sem.at[0])
        table = tabs[...].reshape(n, tabs.shape[2])
        lane = lax.broadcasted_iota(jnp.int32, table.shape, 1)
        within = lane - cap * ((lane * 21846) >> 16)
        local = table - me * parked
        mine = (local >= 0) & (local < parked)
        out_lane = lax.broadcasted_iota(jnp.int32, (n, 128), 1)
        wanted = jnp.zeros((n, 128), jnp.int32)
        for c in range(cap):
            picked = jnp.sum(jnp.where(mine & (within == c), local, 0), axis=1, keepdims=True)
            wanted = jnp.where(out_lane == c, picked, wanted)
        idx_v[...] = wanted
        fetch = pltpu.make_async_copy(idx_v, idx_s, idx_sem)
        fetch.start()

        bulk(q_all, planes - 1, r_sem.at[1])
        line = q_all.at[pl.ds(low * planes, planes)]
        for k in range(1, 4):
            send(line, line, 6, 4 * hi + lax.rem(low + k, 4))
        fetch.wait()
        cache_load.wait()

        for c in range(cap):
            keys[me, c * block : (c + 1) * block, :] = cache[idx_s[me, c]]

        def send_blocks(k, carry):
            to = lax.rem(me + k, n)
            for c in range(cap):
                stage[to, c * block : (c + 1) * block, :] = cache[idx_s[to, c]]
            send(stage.at[to], keys.at[me], 2, to)
            return carry

        lax.fori_loop(1, n, send_blocks, 0)

    pl.run_scoped(first_part, pltpu.VMEM(cache_hbm.shape, BF16))

    bulk(q_all, 3 * planes, r_sem.at[6])
    q_tmp[...] = q_all[...].astype(F32)
    latents = jnp.concatenate(
        [
            jnp.concatenate([q_tmp[:, s * qcols + c, :] for c in range(qcols)], axis=1)
            for s in range(steps)
        ],
        axis=0,
    ).astype(BF16)
    loads[0].wait()
    query = jnp.dot(latents, qup[...], preferred_element_type=F32).astype(BF16).astype(F32)
    loads[1].wait()
    if rows != steps * hl:
        pack[...] = jnp.zeros_like(pack)
    for h in range(hl):
        at = h * head_w
        absorbed = jnp.dot(
            query[:, at : at + nope].astype(BF16), kup[h], preferred_element_type=F32
        )
        for s in range(steps):
            pack[:, s * hl + h, 0:latent] = absorbed[s * n : (s + 1) * n]
            pack[:, s * hl + h, latent:width] = query[s * n : (s + 1) * n, at + nope : at + head_w]
    q_recv[me] = pack[place_of(me)].astype(BF16)

    def on_side(i, k):
        which = side + i - 2 * side * i
        return which * half + lax.rem(inside_side + k, half)

    def send_absorbed(i):
        def one(k, carry):
            to = on_side(i, k)
            q_send[to] = pack[place_of(to)].astype(BF16)
            send(q_send.at[to], q_recv.at[me], 3 + 4 * i, to)
            return carry

        lax.fori_loop(1 - i, half, one, 0)

    send_absorbed(1)
    send_absorbed(0)

    token = lax.broadcasted_iota(jnp.int32, (1, toks), 1)

    def place(k, position):
        first = tab_smem[0, cap * k] // parked * run
        inside = (token >= first) & (token < first + run)
        return jnp.where(inside, token - first + k * run, position)

    position = lax.fori_loop(0, n, place, token)


    owners = max(128 // n, 1)
    group_rows = owners * rows
    row_in = lax.broadcasted_iota(jnp.int32, (group_rows, 1), 0) & (rows - 1)
    second = row_in >= hl
    last = len_smem[0] + second.astype(jnp.int32)
    quarter = (width - latent) // 2
    lane64 = lax.broadcasted_iota(jnp.int32, (8, 2 * quarter), 1)
    upper = lane64 >= quarter
    exponent = (lane64 - jnp.where(upper, quarter, 0)).astype(F32)
    angle = (len_smem[0] + lax.broadcasted_iota(jnp.int32, lane64.shape, 0)).astype(F32) * jnp.exp(
        exponent * (-math.log(10000.0) / quarter)
    )
    cosines, sines = jnp.cos(angle), jnp.sin(angle)
    sines = jnp.where(upper, sines, -sines)
    cosine = jnp.where(second, cosines[1:2], cosines[0:1])
    sine = jnp.where(second, sines[1:2], sines[0:1])

    def attend(first, carry):
        q = q_recv[pl.ds(first, owners)].reshape(group_rows, width)
        kv = keys[...].reshape(toks, width)
        x = q[:, latent:].astype(F32)
        swapped = jnp.concatenate([x[:, quarter:], x[:, :quarter]], axis=1)
        rotated = (x * cosine + swapped * sine).astype(BF16)
        full = jnp.concatenate([q[:, :latent], rotated], axis=1)
        scores = lax.dot_general(
            full, kv, (((1,), (1,)), ((), ())), preferred_element_type=F32
        ) * softmax_scale
        scores = jnp.where(position <= last, scores, big_negative)
        terms = jnp.exp(scores - jnp.max(scores, axis=1, keepdims=True))
        weights = (terms / jnp.sum(terms, axis=1, keepdims=True)).astype(BF16)
        result = jnp.dot(weights, kv[:, :latent], preferred_element_type=F32).astype(BF16)
        l_send[pl.ds(first, owners)] = result.reshape(owners, rows, latent)
        return carry

    bulk(keys, n - 1, r_sem.at[2])
    for i in range(2):
        bulk(q_recv, half - 1 + i, r_sem.at[3 + 4 * i])
        base = (side + i - 2 * side * i) * half
        lax.fori_loop(
            0, half // owners, lambda g, carry: attend(base + g * owners, carry), 0
        )
        if i == 0:
            l_recv[me] = l_send[me]

        def send_latent(k, carry):
            to = on_side(i, k)
            send(l_send.at[to], l_recv.at[me], 4, to)
            return carry

        lax.fori_loop(1 - i, half, send_latent, 0)

    bulk(l_recv, n - 1, r_sem.at[4])
    pack[:, :, 0:latent] = l_recv[...].astype(F32)
    loads[2].wait()

    def per_head(h):
        taken = jnp.concatenate(
            [pack[:, s * hl + h, 0:latent] for s in range(steps)], axis=0
        ).astype(BF16)
        return jnp.dot(taken, vup[h], preferred_element_type=F32)

    values = jnp.concatenate([per_head(h) for h in range(hl)], axis=1)
    wide = values.shape[1]
    both = jnp.stack([values[:n], values[n:]], axis=1)
    both = both.reshape(planes, 4, 2, wide)
    both = jnp.concatenate([both[:, 0], both[:, 2], both[:, 1], both[:, 3]], axis=0)
    both = both.reshape(2 * n, wide)
    values = both.astype(BF16)
    loads[3].wait()

    across = low // 2
    other = me + 2 - 4 * across

    def last_part(part, mid):
        def pair_copy(j):
            return pltpu.make_async_remote_copy(
                src_ref=part.at[j, pl.ds(pl.multiple_of((1 - core) * n, 8), n)],
                dst_ref=part_in.at[j],
                send_sem=pair_s.at[j], recv_sem=pair_r.at[j],
                device_id=(group, pair), device_id_type=MESH,
            )

        def mid_copy(j):
            return pltpu.make_async_remote_copy(
                src_ref=mid.at[j, pl.ds(pl.multiple_of((1 - across) * half, 8), half)],
                dst_ref=mid_in.at[j],
                send_sem=mid_s.at[j], recv_sem=mid_r.at[j],
                device_id=(group, other), device_id_type=MESH,
            )

        def project(j, carry):
            @pl.when(j < chunks)
            def _():
                at = pl.multiple_of(j * cols, 128)
                part[j] = jnp.dot(values, ow[:, pl.ds(at, cols)], preferred_element_type=F32)
                pair_copy(j).start()

            @pl.when((j > 0) & (j < chunks + 1))
            def _():
                i = j - 1
                pair_copy(i).wait_recv()
                mid[i] = part[i, pl.ds(pl.multiple_of(core * n, 8), n)] + part_in[i]
                mid_copy(i).start()

            @pl.when(j > 1)
            def _():
                i = j - 2
                mid_copy(i).wait_recv()
                own = mid[i, pl.ds(pl.multiple_of(across * half, 8), half)] + mid_in[i]
                rs_send[i] = own.reshape(planes, 2, cols)
                rs_recv[hi, i] = rs_send[i, hi]

                def scatter(k, c2):
                    to = lax.rem(hi + k, planes)
                    send(rs_send.at[i, to], rs_recv.at[hi, i], 5, 4 * to + low)
                    return c2

                lax.fori_loop(1, planes, scatter, 0)

            return carry

        lax.fori_loop(0, chunks + 2, project, 0)
        for j in range(chunks):
            pair_copy(j).wait_send()
            mid_copy(j).wait_send()

    pl.run_scoped(
        last_part, pltpu.VMEM((chunks, 2 * n, cols), F32), pltpu.VMEM((chunks, n, cols), F32)
    )

    bulk(rs_recv, planes - 1, r_sem.at[5])
    for j in range(chunks):
        total = rs_recv[0, j]
        for k in range(1, planes):
            total = total + rs_recv[k, j]
        out_ref[:, j * cols : (j + 1) * cols] = total.astype(BF16)

    bulk(tabs, n - 1, s_sem.at[0])
    bulk(q_all, planes - 1, s_sem.at[1])
    bulk(q_all, 3 * planes, s_sem.at[6])
    bulk(stage, n - 1, s_sem.at[2])
    bulk(q_send, half - 1, s_sem.at[3])
    bulk(q_send, half, s_sem.at[7])
    bulk(l_send, n - 1, s_sem.at[4])
    bulk(rs_recv, planes - 1, s_sem.at[5])


def on_device(
    q_latent, latent_cache, block_table, lengths, query_up, key_up, value_up, output_weight
):
    n = lax.axis_size("seq")
    steps, _, ql = q_latent.shape
    parked, block, width = latent_cache.shape
    slots = block_table.shape[1]
    hl, nope, latent = key_up.shape
    vdim = value_up.shape[2]
    d = output_weight.shape[1]
    cap = parked // n
    rows = -(-steps * hl // 16) * 16
    tab_w = -(-slots // 128) * 128
    q_rows = -(-steps * ql // 128 // 16) * 16
    chunks = 7
    cols = d // chunks
    half = n // 2
    run = cap * block

    vmem = pl.BlockSpec(memory_space=pltpu.VMEM)
    smem = pl.BlockSpec(memory_space=pltpu.SMEM)
    hbm = pl.BlockSpec(memory_space=pl.ANY)
    out = pl.pallas_call(
        functools.partial(kernel, n, hl, cap, chunks),
        out_shape=jax.ShapeDtypeStruct((steps, d), BF16),
        in_specs=[vmem, hbm, vmem, smem, smem, hbm, hbm, hbm, hbm],
        out_specs=vmem,
        scratch_shapes=[
            pltpu.VMEM(query_up.shape, BF16),
            pltpu.VMEM(key_up.shape, BF16),
            pltpu.VMEM(value_up.shape, BF16),
            pltpu.VMEM(output_weight.shape, BF16),
            pltpu.VMEM((n, 1, tab_w), jnp.int32),
            pltpu.VMEM((n, 128), jnp.int32),
            pltpu.SMEM((n, 128), jnp.int32),
            pltpu.VMEM((q_rows, 128), BF16),
            pltpu.VMEM((n, q_rows, 128), BF16),
            pltpu.VMEM((n, q_rows, 128), F32),
            pltpu.VMEM((n, run, width), BF16),
            pltpu.VMEM((n, run, width), BF16),
            pltpu.VMEM((n, rows, width), F32),
            pltpu.VMEM((n, rows, width), BF16),
            pltpu.VMEM((n, rows, width), BF16),
            pltpu.VMEM((n, rows, latent), BF16),
            pltpu.VMEM((n, rows, latent), BF16),
            pltpu.VMEM((chunks, n, cols), F32),
            pltpu.VMEM((chunks, half, cols), F32),
            pltpu.VMEM((chunks, n // 4, steps, cols), F32),
            pltpu.VMEM((n // 4, chunks, steps, cols), F32),
            pltpu.SemaphoreType.DMA((5,)),
            pltpu.SemaphoreType.DMA,
            pltpu.SemaphoreType.DMA((8,)),
            pltpu.SemaphoreType.DMA((8,)),
            pltpu.SemaphoreType.DMA((chunks,)),
            pltpu.SemaphoreType.DMA((chunks,)),
            pltpu.SemaphoreType.DMA((chunks,)),
            pltpu.SemaphoreType.DMA((chunks,)),
        ],
        compiler_params=pltpu.CompilerParams(
            collective_id=0, has_side_effects=True, vmem_limit_bytes=61 * 1024 * 1024
        ),
    )(
        q_latent.reshape(steps, ql), latent_cache, block_table, block_table, lengths,
        query_up, key_up, value_up, output_weight,
    )
    return out[:, None, :]


def solution(mesh):
    in_specs = (
        P(None, ("groups", "seq"), None),
        P(("groups", "seq"), None, None),
        P(("groups", "seq"), None),
        P(("groups", "seq")),
        P(None, "seq"),
        P("seq", None, None),
        P("seq", None, None),
        P("seq", None),
    )
    out_specs = P(None, ("groups", "seq"), None)
    return jax.shard_map(
        on_device, mesh=mesh, in_specs=in_specs, out_specs=out_specs, check_vma=False
    )
```

```python
import functools
import math

import jax
import jax.numpy as jnp
from jax import lax
from jax.experimental import pallas as pl
from jax.experimental.pallas import tpu as pltpu
from jax.sharding import PartitionSpec as P

softmax_scale = 0.13524
big_negative = -1e30
F32 = jnp.float32
BF16 = jnp.bfloat16
MESH = pl.DeviceIdType.MESH


def kernel(
    n, hl, cap, chunks,
    q_ref, cache_hbm, tab_ref, tab_smem, len_smem, qup_hbm, kup_hbm, vup_hbm, ow_hbm,
    out_ref,
    qup, kup, vup, ow, tabs, idx_v, idx_s, q_own, q_all, q_tmp, stage, keys,
    pack, q_send, q_recv, l_send, l_recv, part_in, mid_in, rs_send, rs_recv,
    w_sem, idx_sem, s_sem, r_sem, pair_s, pair_r, mid_s, mid_r,
):
    me = lax.axis_index("seq")
    group = lax.axis_index("groups")
    steps = 2
    width = cache_hbm.shape[2]
    latent = kup.shape[2]
    nope = kup.shape[1]
    head_w = nope + width - latent
    block = cache_hbm.shape[1]
    parked = cache_hbm.shape[0]
    slots = tab_ref.shape[1]
    rows = q_send.shape[1]
    half = n // 2
    cols = part_in.shape[2]
    run = cap * block
    toks = n * run
    qcols = q_ref.shape[1] // 128
    core = lax.rem(me, 2)
    pair = me + 1 - 2 * core
    planes = n // 4
    low, hi = lax.rem(me, 4), me // 4
    side, inside_side = me // half, lax.rem(me, half)

    def place_of(device):
        return lax.rem(device, 4) * planes + device // 4


    loads = [
        pltpu.make_async_copy(qup_hbm, qup, w_sem.at[1]),
        pltpu.make_async_copy(kup_hbm, kup, w_sem.at[2]),
        pltpu.make_async_copy(vup_hbm, vup, w_sem.at[3]),
        pltpu.make_async_copy(ow_hbm, ow, w_sem.at[4]),
    ]

    def send(src, dst, phase, to):
        pltpu.make_async_remote_copy(
            src_ref=src, dst_ref=dst, send_sem=s_sem.at[phase], recv_sem=r_sem.at[phase],
            device_id=(group, to), device_id_type=MESH,
        ).start()

    def bulk(buf, count, sem):
        piece = buf.at[pl.ds(0, count)]
        pltpu.make_async_copy(piece, piece, sem).wait()

    def first_part(cache):
        cache_load = pltpu.make_async_copy(cache_hbm, cache, w_sem.at[0])
        cache_load.start()
        for load in loads:
            load.start()

        barrier = pltpu.get_barrier_semaphore()

        def greet(k, carry):
            pl.semaphore_signal(
                barrier, inc=1, device_id=(group, lax.rem(me + k, n)), device_id_type=MESH
            )
            return carry

        lax.fori_loop(1, n, greet, 0)

        tabs[me] = jnp.full((1, tabs.shape[2]), -1, jnp.int32)
        tabs[me, :, 0:slots] = tab_ref[...]
        q_tmp[0] = jnp.zeros_like(q_tmp[0])
        for s in range(steps):
            row = q_ref[s : s + 1, :].astype(F32)
            for c in range(qcols):
                r = s * qcols + c
                q_tmp[0, r : r + 1, :] = row[:, c * 128 : (c + 1) * 128]
        q_own[...] = q_tmp[0].astype(BF16)
        q_all[place_of(me)] = q_own[...]

        pl.semaphore_wait(barrier, n - 1)

        def send_small(k, carry):
            to = lax.rem(me + k, n)
            send(tabs.at[me], tabs.at[me], 0, to)
            return carry

        lax.fori_loop(1, n, send_small, 0)

        def send_query(k, carry):
            to = 4 * lax.rem(hi + k, planes) + low
            send(q_own, q_all.at[place_of(me)], 1, to)
            return carry

        lax.fori_loop(1, planes, send_query, 0)

        bulk(tabs, n - 1, r_sem.at[0])
        table = tabs[...].reshape(n, tabs.shape[2])
        lane = lax.broadcasted_iota(jnp.int32, table.shape, 1)
        within = lane - cap * ((lane * 21846) >> 16)
        local = table - me * parked
        mine = (local >= 0) & (local < parked)
        out_lane = lax.broadcasted_iota(jnp.int32, (n, 128), 1)
        wanted = jnp.zeros((n, 128), jnp.int32)
        for c in range(cap):
            picked = jnp.sum(jnp.where(mine & (within == c), local, 0), axis=1, keepdims=True)
            wanted = jnp.where(out_lane == c, picked, wanted)
        idx_v[...] = wanted
        fetch = pltpu.make_async_copy(idx_v, idx_s, idx_sem)
        fetch.start()

        bulk(q_all, planes - 1, r_sem.at[1])
        line = q_all.at[pl.ds(low * planes, planes)]
        for k in range(1, 4):
            send(line, line, 6, 4 * hi + lax.rem(low + k, 4))
        fetch.wait()
        cache_load.wait()

        for c in range(cap):
            keys[me, c * block : (c + 1) * block, :] = cache[idx_s[me, c]]

        def send_blocks(k, carry):
            to = lax.rem(me + k, n)
            for c in range(cap):
                stage[to, c * block : (c + 1) * block, :] = cache[idx_s[to, c]]
            send(stage.at[to], keys.at[me], 2, to)
            return carry

        lax.fori_loop(1, n, send_blocks, 0)

    pl.run_scoped(first_part, pltpu.VMEM(cache_hbm.shape, BF16))

    bulk(q_all, 3 * planes, r_sem.at[6])
    q_tmp[...] = q_all[...].astype(F32)
    latents = jnp.concatenate(
        [
            jnp.concatenate([q_tmp[:, s * qcols + c, :] for c in range(qcols)], axis=1)
            for s in range(steps)
        ],
        axis=0,
    ).astype(BF16)
    loads[0].wait()
    query = jnp.dot(latents, qup[...], preferred_element_type=F32).astype(BF16).astype(F32)
    loads[1].wait()
    if rows != steps * hl:
        pack[...] = jnp.zeros_like(pack)
    for h in range(hl):
        at = h * head_w
        absorbed = jnp.dot(
            query[:, at : at + nope].astype(BF16), kup[h], preferred_element_type=F32
        )
        for s in range(steps):
            pack[:, s * hl + h, 0:latent] = absorbed[s * n : (s + 1) * n]
            pack[:, s * hl + h, latent:width] = query[s * n : (s + 1) * n, at + nope : at + head_w]
    q_recv[me] = pack[place_of(me)].astype(BF16)

    def on_side(i, k):
        which = side + i - 2 * side * i
        return which * half + lax.rem(inside_side + k, half)

    def send_absorbed(i):
        def one(k, carry):
            to = on_side(i, k)
            q_send[to] = pack[place_of(to)].astype(BF16)
            send(q_send.at[to], q_recv.at[me], 3 + 4 * i, to)
            return carry

        lax.fori_loop(1 - i, half, one, 0)

    send_absorbed(1)
    send_absorbed(0)

    token = lax.broadcasted_iota(jnp.int32, (1, toks), 1)

    def place(k, position):
        first = tab_smem[0, cap * k] // parked * run
        inside = (token >= first) & (token < first + run)
        return jnp.where(inside, token - first + k * run, position)

    position = lax.fori_loop(0, n, place, token)


    owners = max(128 // n, 1)
    group_rows = owners * rows
    row_in = lax.broadcasted_iota(jnp.int32, (group_rows, 1), 0) & (rows - 1)
    second = row_in >= hl
    last = len_smem[0] + second.astype(jnp.int32)
    quarter = (width - latent) // 2
    lane64 = lax.broadcasted_iota(jnp.int32, (8, 2 * quarter), 1)
    upper = lane64 >= quarter
    exponent = (lane64 - jnp.where(upper, quarter, 0)).astype(F32)
    angle = (len_smem[0] + lax.broadcasted_iota(jnp.int32, lane64.shape, 0)).astype(F32) * jnp.exp(
        exponent * (-math.log(10000.0) / quarter)
    )
    cosines, sines = jnp.cos(angle), jnp.sin(angle)
    sines = jnp.where(upper, sines, -sines)
    cosine = jnp.where(second, cosines[1:2], cosines[0:1])
    sine = jnp.where(second, sines[1:2], sines[0:1])

    def attend(first, carry):
        q = q_recv[pl.ds(first, owners)].reshape(group_rows, width)
        kv = keys[...].reshape(toks, width)
        x = q[:, latent:].astype(F32)
        swapped = jnp.concatenate([x[:, quarter:], x[:, :quarter]], axis=1)
        rotated = (x * cosine + swapped * sine).astype(BF16)
        full = jnp.concatenate([q[:, :latent], rotated], axis=1)
        scores = lax.dot_general(
            full, kv, (((1,), (1,)), ((), ())), preferred_element_type=F32
        ) * softmax_scale
        scores = jnp.where(position <= last, scores, big_negative)
        terms = jnp.exp(scores - jnp.max(scores, axis=1, keepdims=True))
        weights = (terms / jnp.sum(terms, axis=1, keepdims=True)).astype(BF16)
        result = jnp.dot(weights, kv[:, :latent], preferred_element_type=F32).astype(BF16)
        l_send[pl.ds(first, owners)] = result.reshape(owners, rows, latent)
        return carry

    bulk(keys, n - 1, r_sem.at[2])
    for i in range(2):
        bulk(q_recv, half - 1 + i, r_sem.at[3 + 4 * i])
        base = (side + i - 2 * side * i) * half
        lax.fori_loop(
            0, half // owners, lambda g, carry: attend(base + g * owners, carry), 0
        )
        if i == 0:
            l_recv[me] = l_send[me]

        def send_latent(k, carry):
            to = on_side(i, k)
            send(l_send.at[to], l_recv.at[me], 4, to)
            return carry

        lax.fori_loop(1 - i, half, send_latent, 0)

    bulk(l_recv, n - 1, r_sem.at[4])
    pack[:, :, 0:latent] = l_recv[...].astype(F32)
    loads[2].wait()

    def per_head(h):
        taken = jnp.concatenate(
            [pack[:, s * hl + h, 0:latent] for s in range(steps)], axis=0
        ).astype(BF16)
        return jnp.dot(taken, vup[h], preferred_element_type=F32)

    values = jnp.concatenate([per_head(h) for h in range(hl)], axis=1)
    wide = values.shape[1]
    both = jnp.stack([values[:n], values[n:]], axis=1)
    both = both.reshape(planes, 4, 2, wide)
    both = jnp.concatenate([both[:, 0], both[:, 2], both[:, 1], both[:, 3]], axis=0)
    both = both.reshape(2 * n, wide)
    values = both.astype(BF16)
    loads[3].wait()

    across = low // 2
    other = me + 2 - 4 * across

    def last_part(part, mid):
        def pair_copy(j):
            return pltpu.make_async_remote_copy(
                src_ref=part.at[j, pl.ds(pl.multiple_of((1 - core) * n, 8), n)],
                dst_ref=part_in.at[j],
                send_sem=pair_s.at[j], recv_sem=pair_r.at[j],
                device_id=(group, pair), device_id_type=MESH,
            )

        def mid_copy(j):
            return pltpu.make_async_remote_copy(
                src_ref=mid.at[j, pl.ds(pl.multiple_of((1 - across) * half, 8), half)],
                dst_ref=mid_in.at[j],
                send_sem=mid_s.at[j], recv_sem=mid_r.at[j],
                device_id=(group, other), device_id_type=MESH,
            )

        def project(j, carry):
            @pl.when(j < chunks)
            def _():
                at = pl.multiple_of(j * cols, 128)
                part[j] = jnp.dot(values, ow[:, pl.ds(at, cols)], preferred_element_type=F32)
                pair_copy(j).start()

            @pl.when((j > 1) & (j < chunks + 2))
            def _():
                i = j - 2
                pair_copy(i).wait_recv()
                mid[i] = part[i, pl.ds(pl.multiple_of(core * n, 8), n)] + part_in[i]
                mid_copy(i).start()

            @pl.when(j > 3)
            def _():
                i = j - 4
                mid_copy(i).wait_recv()
                own = mid[i, pl.ds(pl.multiple_of(across * half, 8), half)] + mid_in[i]
                rs_send[i] = own.reshape(planes, 2, cols)
                rs_recv[hi, i] = rs_send[i, hi]

                def scatter(k, c2):
                    to = lax.rem(hi + k, planes)
                    send(rs_send.at[i, to], rs_recv.at[hi, i], 5, 4 * to + low)
                    return c2

                lax.fori_loop(1, planes, scatter, 0)

            return carry

        lax.fori_loop(0, chunks + 4, project, 0)
        for j in range(chunks):
            pair_copy(j).wait_send()
            mid_copy(j).wait_send()

    pl.run_scoped(
        last_part, pltpu.VMEM((chunks, 2 * n, cols), F32), pltpu.VMEM((chunks, n, cols), F32)
    )

    bulk(rs_recv, planes - 1, r_sem.at[5])
    for j in range(chunks):
        total = rs_recv[0, j]
        for k in range(1, planes):
            total = total + rs_recv[k, j]
        out_ref[:, j * cols : (j + 1) * cols] = total.astype(BF16)

    bulk(tabs, n - 1, s_sem.at[0])
    bulk(q_all, planes - 1, s_sem.at[1])
    bulk(q_all, 3 * planes, s_sem.at[6])
    bulk(stage, n - 1, s_sem.at[2])
    bulk(q_send, half - 1, s_sem.at[3])
    bulk(q_send, half, s_sem.at[7])
    bulk(l_send, n - 1, s_sem.at[4])
    bulk(rs_recv, planes - 1, s_sem.at[5])


def on_device(
    q_latent, latent_cache, block_table, lengths, query_up, key_up, value_up, output_weight
):
    n = lax.axis_size("seq")
    steps, _, ql = q_latent.shape
    parked, block, width = latent_cache.shape
    slots = block_table.shape[1]
    hl, nope, latent = key_up.shape
    vdim = value_up.shape[2]
    d = output_weight.shape[1]
    cap = parked // n
    rows = -(-steps * hl // 16) * 16
    tab_w = -(-slots // 128) * 128
    q_rows = -(-steps * ql // 128 // 16) * 16
    chunks = 7
    cols = d // chunks
    half = n // 2
    run = cap * block

    vmem = pl.BlockSpec(memory_space=pltpu.VMEM)
    smem = pl.BlockSpec(memory_space=pltpu.SMEM)
    hbm = pl.BlockSpec(memory_space=pl.ANY)
    out = pl.pallas_call(
        functools.partial(kernel, n, hl, cap, chunks),
        out_shape=jax.ShapeDtypeStruct((steps, d), BF16),
        in_specs=[vmem, hbm, vmem, smem, smem, hbm, hbm, hbm, hbm],
        out_specs=vmem,
        scratch_shapes=[
            pltpu.VMEM(query_up.shape, BF16),
            pltpu.VMEM(key_up.shape, BF16),
            pltpu.VMEM(value_up.shape, BF16),
            pltpu.VMEM(output_weight.shape, BF16),
            pltpu.VMEM((n, 1, tab_w), jnp.int32),
            pltpu.VMEM((n, 128), jnp.int32),
            pltpu.SMEM((n, 128), jnp.int32),
            pltpu.VMEM((q_rows, 128), BF16),
            pltpu.VMEM((n, q_rows, 128), BF16),
            pltpu.VMEM((n, q_rows, 128), F32),
            pltpu.VMEM((n, run, width), BF16),
            pltpu.VMEM((n, run, width), BF16),
            pltpu.VMEM((n, rows, width), F32),
            pltpu.VMEM((n, rows, width), BF16),
            pltpu.VMEM((n, rows, width), BF16),
            pltpu.VMEM((n, rows, latent), BF16),
            pltpu.VMEM((n, rows, latent), BF16),
            pltpu.VMEM((chunks, n, cols), F32),
            pltpu.VMEM((chunks, half, cols), F32),
            pltpu.VMEM((chunks, n // 4, steps, cols), F32),
            pltpu.VMEM((n // 4, chunks, steps, cols), F32),
            pltpu.SemaphoreType.DMA((5,)),
            pltpu.SemaphoreType.DMA,
            pltpu.SemaphoreType.DMA((8,)),
            pltpu.SemaphoreType.DMA((8,)),
            pltpu.SemaphoreType.DMA((chunks,)),
            pltpu.SemaphoreType.DMA((chunks,)),
            pltpu.SemaphoreType.DMA((chunks,)),
            pltpu.SemaphoreType.DMA((chunks,)),
        ],
        compiler_params=pltpu.CompilerParams(
            collective_id=0, has_side_effects=True, vmem_limit_bytes=61 * 1024 * 1024
        ),
    )(
        q_latent.reshape(steps, ql), latent_cache, block_table, block_table, lengths,
        query_up, key_up, value_up, output_weight,
    )
    return out[:, None, :]


def solution(mesh):
    in_specs = (
        P(None, ("groups", "seq"), None),
        P(("groups", "seq"), None, None),
        P(("groups", "seq"), None),
        P(("groups", "seq")),
        P(None, "seq"),
        P("seq", None, None),
        P("seq", None, None),
        P("seq", None),
    )
    out_specs = P(None, ("groups", "seq"), None)
    return jax.shard_map(
        on_device, mesh=mesh, in_specs=in_specs, out_specs=out_specs, check_vma=False
    )
```
